32 devices in a mesh: st: 4 (over x, core), fifth: 8 (over z, y).
Axes of the slice: x: 2, y: 2, z: 4, core: 2. Of those that a mesh axis runs over, the one named last changes fastest.
Arguments:
- source_field: float32 [2, 4, 3, 8, 4, 4096], P(None, None, None, 'fifth', 'st'), may hold values from -6 to 6
- gauge_rows: float32 [2, 4, 2, 3, 4, 4096], P(None, None, None, None, 'st', 'fifth'), may hold values from -3 to 3
Outputs:
- applied_once: float32 [2, 4, 3, 8, 4, 4096], P(None, None, None, 'fifth', 'st')
- applied_twice: float32 [2, 4, 3, 8, 4, 4096], P(None, None, None, 'fifth', 'st')
The draws below stay inside these ranges and needn't reach their ends.
All inputs are finite; a program needn't handle non-finite values.
Results may differ from the reference program's by a relative error of at most 0.00002.
Values sent between devices are 32-bit elements; how exact they have to be, the bound alone decides.
A program may use at most 64 MiB of HBM per device.

```python
import jax
import jax.numpy as jnp
import numpy as np
from jax import lax

LS = 16
S3 = 4096
NT = 4
L5 = 8


def shard_levels(stream_key, extent, split, least, top_value):
    def one(position, parts):
        draws = jax.random.uniform(jax.random.fold_in(jax.random.fold_in(stream_key, 6), position), (parts,), jnp.float32, least / len(split), top_value / len(split))
        return jnp.repeat(jnp.exp(draws), extent[position] // parts).reshape((-1,) + (1,) * (len(extent) - position - 1))

    loudness = one(*split[0])
    for cut in split[1:]:
        loudness = loudness * one(*cut)
    return loudness


def scatter_about(key, dims, scale, reach, split=(), kind=jnp.bfloat16):
    level = shard_levels(key, dims, split, -0.22, 0.18) if split else 1.0
    drawn = jax.random.normal(key, dims, jnp.float32) * scale * level
    return jnp.minimum(jnp.maximum(drawn, -reach), reach).astype(kind)


def setup_inputs(seed: int = 0) -> dict:
    splits = jax.random.split(jax.random.key(seed), 3)
    source_field = scatter_about(splits[0], (2, 4, 3, L5, NT, S3), 1.0, 6.0, ((3, 8), (4, 4)), jnp.float32)
    gauge_rows = scatter_about(splits[1], (2, 4, 2, 3, NT, S3), 0.45, 3.0, ((4, 4), (5, 8)), jnp.float32)
    return {"source_field": source_field, "gauge_rows": gauge_rows}


def gamma_tables():
    pauli_real = [np.array([[0.0, 1.0], [1.0, 0.0]]), np.zeros((2, 2)), np.array([[1.0, 0.0], [0.0, -1.0]])]
    pauli_imag = [np.zeros((2, 2)), np.array([[0.0, -1.0], [1.0, 0.0]]), np.zeros((2, 2))]
    real_blocks = []
    imag_blocks = []
    for k in range(3):
        real_matrix = np.zeros((4, 4))
        imag_matrix = np.zeros((4, 4))
        real_matrix[0:2, 2:4] = pauli_imag[k]
        imag_matrix[0:2, 2:4] = -pauli_real[k]
        real_matrix[2:4, 0:2] = -pauli_imag[k]
        imag_matrix[2:4, 0:2] = pauli_real[k]
        real_blocks.append(real_matrix)
        imag_blocks.append(imag_matrix)
    timelike = np.zeros((4, 4))
    timelike[0:2, 2:4] = np.eye(2)
    timelike[2:4, 0:2] = np.eye(2)
    real_blocks.append(timelike)
    imag_blocks.append(np.zeros((4, 4)))
    return np.stack(real_blocks), np.stack(imag_blocks)


GAMMA_REAL, GAMMA_IMAG = gamma_tables()
WALL_HEIGHT = 1.8
QUARK_MASS = 0.5


def complete_links(gauge_rows):
    first_real, first_imag = gauge_rows[0, :, 0], gauge_rows[1, :, 0]
    second_real, second_imag = gauge_rows[0, :, 1], gauge_rows[1, :, 1]
    real_parts = []
    imag_parts = []
    for a in range(3):
        b = (a + 1) % 3
        c = (a + 2) % 3
        real_value = (first_real[:, b] * second_real[:, c] - first_imag[:, b] * second_imag[:, c]) - (first_real[:, c] * second_real[:, b] - first_imag[:, c] * second_imag[:, b])
        imag_value = (first_real[:, b] * second_imag[:, c] + first_imag[:, b] * second_real[:, c]) - (first_real[:, c] * second_imag[:, b] + first_imag[:, c] * second_real[:, b])
        real_parts.append(real_value)
        imag_parts.append(-imag_value)
    last_row = jnp.stack([jnp.stack(real_parts, axis=1), jnp.stack(imag_parts, axis=1)])
    return jnp.concatenate([gauge_rows, last_row[:, :, None]], axis=2)


def adjoint(link):
    return jnp.stack([jnp.swapaxes(link[0], 0, 1), -jnp.swapaxes(link[1], 0, 1)])


def colour_product(link, field):
    real_sum = None
    imag_sum = None
    for b in range(3):
        link_real = link[0][:, b][None, :, None]
        link_imag = link[1][:, b][None, :, None]
        field_real = field[0][:, b:b + 1]
        field_imag = field[1][:, b:b + 1]
        real_term = link_real * field_real - link_imag * field_imag
        imag_term = link_real * field_imag + link_imag * field_real
        real_sum = real_term if real_sum is None else real_sum + real_term
        imag_sum = imag_term if imag_sum is None else imag_sum + imag_term
    return jnp.stack([real_sum, imag_sum])


def spin_project(direction, factor, field):
    real_rows = []
    imag_rows = []
    for i in range(4):
        real_value = field[0, i]
        imag_value = field[1, i]
        for j in range(4):
            coeff_real = float(factor * GAMMA_REAL[direction, i, j])
            coeff_imag = float(factor * GAMMA_IMAG[direction, i, j])
            if coeff_real != 0.0:
                real_value = real_value + coeff_real * field[0, j]
                imag_value = imag_value + coeff_real * field[1, j]
            if coeff_imag != 0.0:
                real_value = real_value - coeff_imag * field[1, j]
                imag_value = imag_value + coeff_imag * field[0, j]
        real_rows.append(real_value)
        imag_rows.append(imag_value)
    return jnp.stack([jnp.stack(real_rows), jnp.stack(imag_rows)])


def neighbour(field, stride, offset):
    coords = (jnp.arange(field.shape[-1]) // stride) % LS
    if offset > 0:
        at_edge = coords == LS - 1
        shifted = jnp.roll(field, -stride, axis=-1)
        wrapped = jnp.roll(field, stride * (LS - 1), axis=-1)
    else:
        at_edge = coords == 0
        shifted = jnp.roll(field, stride, axis=-1)
        wrapped = jnp.roll(field, -stride * (LS - 1), axis=-1)
    return jnp.where(at_edge, wrapped, shifted)


def spatial_hops(field, gauge_field):
    summed = None
    for k in range(3):
        stride = LS ** k
        link = gauge_field[:, k]
        forward = neighbour(field, stride, 1)
        behind = neighbour(field, stride, -1)
        back_link = neighbour(link, stride, -1)
        term = colour_product(link, spin_project(k, -1.0, forward)) + colour_product(adjoint(back_link), spin_project(k, 1.0, behind))
        summed = term if summed is None else summed + term
    return summed


def wilson_hops(field, gauge_field):
    summed = spatial_hops(field, gauge_field)
    time_link = gauge_field[:, 3]
    slots = jnp.arange(NT)
    ahead_factor = jnp.where(slots == NT - 1, -1.0, 1.0)[:, None]
    behind_factor = jnp.where(slots == 0, -1.0, 1.0)[:, None]
    forward = jnp.roll(field, -1, axis=4) * ahead_factor
    behind = jnp.roll(field, 1, axis=4) * behind_factor
    back_link = jnp.roll(time_link, 1, axis=3)
    summed = summed + colour_product(time_link, spin_project(3, -1.0, forward))
    summed = summed + colour_product(adjoint(back_link), spin_project(3, 1.0, behind))
    return summed


def apply_dirac(spinor, gauge_field):
    slices = jnp.moveaxis(spinor, 3, 0)
    hopped = lax.map(lambda piece: wilson_hops(piece[:, :, :, None], gauge_field)[:, :, :, 0], slices)
    hopped = jnp.moveaxis(hopped, 0, 3)
    upper_spins = spinor[:, :2]
    lower_spins = spinor[:, 2:]
    fifth = jnp.arange(L5)
    next_factor = jnp.where(fifth == L5 - 1, -QUARK_MASS, 1.0)[:, None, None]
    prev_factor = jnp.where(fifth == 0, -QUARK_MASS, 1.0)[:, None, None]
    next_lower = jnp.roll(lower_spins, -1, axis=3) * next_factor
    prev_upper = jnp.roll(upper_spins, 1, axis=3) * prev_factor
    chiral = jnp.concatenate([prev_upper, next_lower], axis=1)
    return (5.0 - WALL_HEIGHT) * spinor - 0.5 * hopped - chiral


def reference(source_field, gauge_rows):
    gauge_field = complete_links(gauge_rows)
    applied_once = apply_dirac(source_field, gauge_field)
    applied_twice = apply_dirac(applied_once, gauge_field)
    return (applied_once, applied_twice)
```

```python
import functools

import jax
import jax.numpy as jnp
from jax import lax
from jax.experimental import pallas as pl
from jax.experimental.pallas import tpu as pltpu
from jax.sharding import PartitionSpec as P

WALL_HEIGHT = 1.8
QUARK_MASS = 0.5
MESH = pl.DeviceIdType.MESH
LANES = 128
ROWS = 8


def roll(value, shift, axis):
    return pltpu.roll(value, shift % value.shape[axis], axis)


def i_sigma(k, half):
    (r0, r1), (m0, m1) = half
    neg = lambda xs: [-x for x in xs]
    if k == 0:
        return [neg(m1), neg(m0)], [r1, r0]
    if k == 1:
        return [r1, neg(r0)], [m1, neg(m0)]
    return [neg(m0), m1], [r0, neg(r1)]


def combine(a, b, sign):
    op = (lambda x, y: x + y) if sign > 0 else (lambda x, y: x - y)
    return [[[op(x, y) for x, y in zip(sa, sb)] for sa, sb in zip(pa, pb)] for pa, pb in zip(a, b)]


def each(fn, *halves):
    return [
        [[fn(*xs) for xs in zip(*spins)] for spins in zip(*parts)] for parts in zip(*halves)
    ]


def colour_product(link, half, dagger):
    out = [[[None] * 3 for _ in range(2)] for _ in range(2)]
    for a in range(3):
        for b in range(3):
            re = link(0, b, a) if dagger else link(0, a, b)
            im = link(1, b, a) if dagger else link(1, a, b)
            for s in range(2):
                fr, fi = half[0][s][b], half[1][s][b]
                if dagger:
                    tr, ti = re * fr + im * fi, re * fi - im * fr
                else:
                    tr, ti = re * fr - im * fi, re * fi + im * fr
                out[0][s][a] = tr if b == 0 else out[0][s][a] + tr
                out[1][s][a] = ti if b == 0 else out[1][s][a] + ti
    return out


def kernel(n5, nt, rows, src, gauge, once, twice, gath, v_buf, part_buf, links, back, stage_in,
           stage_out, fifth_in, time_out, time_in, raw_in,
           gsend, grecv, lsem, fsend, frecv, tsend, trecv, rsend, rrecv, osem):
    me = lax.axis_index("fifth")
    mt = lax.axis_index("st")
    nxt, prv = lax.rem(me + 1, n5), lax.rem(me + n5 - 1, n5)
    t_nxt, t_prv = lax.rem(mt + 1, nt), lax.rem(mt + nt - 1, nt)
    q, m = me // 2, lax.rem(me, 2)
    nq = n5 // 2
    pair = q * 2 + 1 - m
    shard_rows = 48 * rows
    half_rows = 24 * rows

    load_src = pltpu.make_async_copy(src, stage_in, lsem.at[0])
    load_src.start()
    load_gauge = pltpu.make_async_copy(
        gauge, gath.at[pl.ds(pl.multiple_of(me * shard_rows, 8), shard_rows)], lsem.at[1]
    )
    load_gauge.start()

    barrier = pltpu.get_barrier_semaphore()
    for peer in (nxt, prv, lax.rem(me + 2, n5), lax.rem(me + n5 - 2, n5)):
        pl.semaphore_signal(barrier, inc=1, device_id={"fifth": peer}, device_id_type=MESH)
    for peer in (t_nxt, t_prv):
        pl.semaphore_signal(barrier, inc=1, device_id={"st": peer}, device_id_type=MESH)
    pl.semaphore_wait(barrier, 6)

    def shard(part, b):
        return gath.at[pl.ds(pl.multiple_of(b * shard_rows + part * half_rows, 8), half_rows)]

    def pass_on(part, b, kind, own=False):
        target = (me + 2, me - 2, pair)[kind]
        return pltpu.make_async_remote_copy(
            src_ref=gauge.at[pl.ds(part * half_rows, half_rows)] if own else shard(part, b),
            dst_ref=shard(part, b),
            send_sem=gsend.at[part, b, kind],
            recv_sem=grecv.at[part, b],
            device_id={"fifth": target},
            device_id_type=MESH,
        )

    def arrived(part, b):
        pass_on(part, b, 2).wait_recv()

    has_up, has_down = q + 1 < nq, q > 0

    pass_on(1, me, 2, True).start()
    pass_on(0, me, 2, True).start()

    @pl.when(has_up)
    def _():
        pass_on(0, me, 0, True).start()
        pass_on(1, me, 0, True).start()

    @pl.when(has_down)
    def _():
        pass_on(0, me, 1, True).start()
        pass_on(1, me, 1, True).start()

    def raw_copy(which):
        return pltpu.make_async_remote_copy(
            src_ref=src.at[:, pl.ds(6 * which, 6)],
            dst_ref=raw_in.at[which],
            send_sem=rsend.at[which],
            recv_sem=rrecv.at[which],
            device_id={"fifth": (nxt, prv)[which]},
            device_id_type=MESH,
        )

    raw_copy(0).start()
    raw_copy(1).start()

    def fifth_copy(which, j):
        return pltpu.make_async_remote_copy(
            src_ref=v_buf.at[1, j, :, pl.ds(6 * which, 6)],
            dst_ref=fifth_in.at[which, j],
            send_sem=fsend.at[which, j],
            recv_sem=frecv.at[which, j],
            device_id={"fifth": (nxt, prv)[which]},
            device_id_type=MESH,
        )

    def time_copy(phase, which, j):
        return pltpu.make_async_remote_copy(
            src_ref=time_out.at[phase, which, j],
            dst_ref=time_in.at[phase, which, j],
            send_sem=tsend.at[phase, which, j],
            recv_sem=trecv.at[phase, which, j],
            device_id={"st": (t_prv, t_nxt)[which]},
            device_id_type=MESH,
        )

    def load_half(ref, base):
        return [[[ref(p, base + 3 * s + c) for c in range(3)] for s in range(2)] for p in range(2)]

    def put_half(ref, half):
        for p in range(2):
            for s in range(2):
                for c in range(3):
                    ref[p, 3 * s + c] = half[p][s][c]

    load_src.wait()

    @pl.loop(0, 4)
    def _(j):
        for p in range(2):
            for c in range(12):
                v_buf[0, j, p, c] = stage_in[p, c, pl.ds(j, ROWS, stride=4), :]
        get = lambda p, c: v_buf[0, j, p, c]
        put_half(time_out.at[0, 0, j], combine(load_half(get, 0), load_half(get, 6), -1))
        time_copy(0, 0, j).start()

    arrived(1, pair)

    @pl.when(has_up)
    def _():
        pass_on(1, pair, 0).start()

    @pl.when(has_down)
    def _():
        pass_on(1, pair, 1).start()

    @pl.loop(1, nq)
    def _(k):
        below, above = me - 2 * k, me + 2 * k
        pair_below, pair_above = pair - 2 * k, pair + 2 * k

        @pl.when(q - k >= 0)
        def _():
            arrived(0, below)
            pass_on(0, below, 2).start()

            @pl.when(has_up)
            def _():
                pass_on(0, below, 0).start()

        @pl.when(q + k < nq)
        def _():
            arrived(0, above)
            pass_on(0, above, 2).start()

            @pl.when(has_down)
            def _():
                pass_on(0, above, 1).start()

        for b_low, b_high in ((below, above), (pair_below, pair_above)):

            @pl.when(q - k >= 0)
            def _():
                arrived(1, b_low)

                @pl.when(has_up)
                def _():
                    pass_on(1, b_low, 0).start()

            @pl.when(q + k < nq)
            def _():
                arrived(1, b_high)

                @pl.when(has_down)
                def _():
                    pass_on(1, b_high, 1).start()

    @pl.loop(0, nq)
    def _(k):
        arrived(0, 2 * k + 1 - m)

    load_gauge.wait()

    @pl.loop(0, 4)
    def _(j):
        offset = (j // rows) * shard_rows + lax.rem(j, rows)

        for mu in range(4):
            u = [[[None] * 3 for _ in range(3)] for _ in range(2)]
            for p in range(2):
                for a in range(2):
                    for b in range(3):
                        comp = ((p * 4 + mu) * 2 + a) * 3 + b
                        u[p][a][b] = gath[pl.ds(offset + comp * rows, ROWS, stride=192), :]
            (r0, r1, _), (m0, m1, _) = u
            for a in range(3):
                b, c = (a + 1) % 3, (a + 2) % 3
                u[0][2][a] = (r0[b] * r1[c] - m0[b] * m1[c]) - (r0[c] * r1[b] - m0[c] * m1[b])
                u[1][2][a] = (r0[c] * m1[b] + m0[c] * r1[b]) - (r0[b] * m1[c] + m0[b] * r1[c])
            for p in range(2):
                for a in range(3):
                    for b in range(3):
                        links[j, mu, p, 3 * a + b] = u[p][a][b]

    def time_link(j):
        return lambda p, a, b: links[j, 3, p, 3 * a + b]

    def send_behind(phase, j, get):
        total = combine(load_half(get, 0), load_half(get, 6), 1)
        put_half(time_out.at[phase, 1, j], colour_product(time_link(j), total, True))
        time_copy(phase, 1, j).start()

    @pl.loop(0, 4)
    def _(j):
        send_behind(0, j, lambda p, c: v_buf[0, j, p, c])

    lane = lax.broadcasted_iota(jnp.int32, (ROWS, LANES), 1)
    x = lax.rem(lane, 16)

    def xor1(j):
        return j + 1 - 2 * lax.rem(j, 2)

    def xor2(j):
        return lax.rem(j + 2, 4)

    def shift(k, ahead, j, here, there):
        if k == 0:
            if ahead:
                return jnp.where(x == 15, roll(here, 15, 1), roll(here, -1, 1))
            return jnp.where(x == 0, roll(here, -15, 1), roll(here, 1, 1))
        if k == 1:
            if ahead:
                return roll(jnp.where(lane >= 16, here, there), -16, 1)
            return roll(jnp.where(lane < LANES - 16, here, there), 16, 1)
        if ahead:
            return jnp.where(j >= 2, roll(there, -1, 0), there)
        return jnp.where(j < 2, roll(there, 1, 0), there)

    @pl.loop(0, 4)
    def _(j):
        other = (j, xor1(j), xor2(j))
        for k in range(3):
            for p in range(2):
                for c in range(9):
                    back[j, k, p, c] = shift(
                        k, False, j, links[j, k, p, c], links[other[k], k, p, c]
                    )

    time_last = jnp.where(mt == nt - 1, -1.0, 1.0).astype(jnp.float32)
    time_first = jnp.where(mt == 0, -1.0, 1.0).astype(jnp.float32)
    fifth_last = jnp.where(me == n5 - 1, -QUARK_MASS, 1.0).astype(jnp.float32)
    fifth_first = jnp.where(me == 0, -QUARK_MASS, 1.0).astype(jnp.float32)

    def local_part(phase):
        @pl.loop(0, 4)
        def _(j):
            other = (j, xor1(j), xor2(j))
            for k in range(3):

                def halves(at):
                    get = lambda p, c: v_buf[phase, at, p, c]
                    upper, turned = load_half(get, 0), i_sigma_lists(k, load_half(get, 6))
                    return combine(upper, turned, 1), combine(upper, turned, -1)

                there_plus, there_minus = halves(other[k])
                here_plus, here_minus = halves(j) if k == 1 else (there_plus, there_minus)
                go = lambda ahead: lambda h, t: shift(k, ahead, j, h, t)
                ahead_half = each(go(True), here_plus, there_plus)
                behind_half = each(go(False), here_minus, there_minus)
                moved_ahead = colour_product(
                    lambda p, a, b: links[j, k, p, 3 * a + b], ahead_half, False
                )
                moved_behind = colour_product(
                    lambda p, a, b: back[j, k, p, 3 * a + b], behind_half, True
                )
                upper = combine(moved_ahead, moved_behind, 1)
                lower = i_sigma_lists(k, combine(moved_behind, moved_ahead, -1))
                for base, half in ((0, upper), (6, lower)):
                    for p in range(2):
                        for s in range(2):
                            for c in range(3):
                                i = base + 3 * s + c
                                old = (
                                    (5.0 - WALL_HEIGHT) * v_buf[phase, j, p, i]
                                    if k == 0
                                    else part_buf[j, p, i]
                                )
                                part_buf[j, p, i] = old - 0.5 * half[p][s][c]

    def finish(phase):
        @pl.loop(0, 4)
        def _(j):
            time_copy(phase, 0, j).wait_recv()
            time_copy(phase, 1, j).wait_recv()
            if phase == 1:
                fifth_copy(0, j).wait_recv()
                fifth_copy(1, j).wait_recv()
            ahead = load_half(lambda p, c: time_in[phase, 0, j, p, c] * time_last, 0)
            behind = load_half(lambda p, c: time_in[phase, 1, j, p, c] * time_first, 0)
            moved = colour_product(time_link(j), ahead, False)
            upper = combine(moved, behind, 1)
            lower = combine(behind, moved, -1)
            for which, half in ((0, upper), (1, lower)):
                for p in range(2):
                    for s in range(2):
                        for c in range(3):
                            i = 3 * s + c
                            if phase == 0:
                                chiral = raw_in[which, p, i, pl.ds(j, ROWS, stride=4), :]
                            else:
                                chiral = fifth_in[which, j, p, i]
                            chiral = chiral * (fifth_first, fifth_last)[which]
                            value = part_buf[j, p, 6 * which + i] - 0.5 * half[p][s][c] - chiral
                            stage_out[phase, p, 6 * which + i, pl.ds(j, ROWS, stride=4), :] = value
                            if phase == 0:
                                v_buf[1, j, p, 6 * which + i] = value
            if phase == 0:
                fifth_copy(0, j).start()
                fifth_copy(1, j).start()
                get = lambda p, c: v_buf[1, j, p, c]
                put_half(time_out.at[1, 0, j], combine(load_half(get, 0), load_half(get, 6), -1))
                time_copy(1, 0, j).start()
                send_behind(1, j, get)

    local_part(0)
    raw_copy(0).wait_recv()
    raw_copy(1).wait_recv()
    finish(0)
    write_once = pltpu.make_async_copy(stage_out.at[0], once, osem.at[0])
    write_once.start()
    local_part(1)
    finish(1)
    write_twice = pltpu.make_async_copy(stage_out.at[1], twice, osem.at[1])
    write_twice.start()

    raw_copy(0).wait_send()
    raw_copy(1).wait_send()

    @pl.loop(0, 4)
    def _(j):
        for which in range(2):
            fifth_copy(which, j).wait_send()
            time_copy(0, which, j).wait_send()
            time_copy(1, which, j).wait_send()

    for b in (me, pair):

        @pl.when(has_up)
        def _():
            pass_on(1, b, 0).wait_send()

        @pl.when(has_down)
        def _():
            pass_on(1, b, 1).wait_send()

    pass_on(1, me, 2).wait_send()
    pass_on(0, me, 2).wait_send()

    @pl.when(has_up)
    def _():
        pass_on(0, me, 0).wait_send()

    @pl.when(has_down)
    def _():
        pass_on(0, me, 1).wait_send()

    @pl.loop(1, nq)
    def _(k):
        below, above = me - 2 * k, me + 2 * k
        pair_below, pair_above = pair - 2 * k, pair + 2 * k

        @pl.when(q - k >= 0)
        def _():
            pass_on(0, below, 2).wait_send()

            @pl.when(has_up)
            def _():
                pass_on(0, below, 0).wait_send()
                pass_on(1, below, 0).wait_send()
                pass_on(1, pair_below, 0).wait_send()

        @pl.when(q + k < nq)
        def _():
            pass_on(0, above, 2).wait_send()

            @pl.when(has_down)
            def _():
                pass_on(0, above, 1).wait_send()
                pass_on(1, above, 1).wait_send()
                pass_on(1, pair_above, 1).wait_send()

    write_once.wait()
    write_twice.wait()


def i_sigma_lists(k, half):
    return [list(part) for part in i_sigma(k, half)]


def on_device(n5, nt, source_field, gauge_rows):
    rows = gauge_rows.shape[-1] // LANES
    src = source_field.reshape(2, 12, 32, LANES)
    gauge = gauge_rows.reshape(48 * rows, LANES)
    field = jax.ShapeDtypeStruct((2, 12, 32, LANES), jnp.float32)
    f32 = lambda *shape: pltpu.VMEM(shape, jnp.float32)
    sem = lambda *shape: pltpu.SemaphoreType.DMA(shape)
    once, twice = pl.pallas_call(
        functools.partial(kernel, n5, nt, rows),
        out_shape=(field, field),
        in_specs=[pl.BlockSpec(memory_space=pl.ANY)] * 2,
        out_specs=[pl.BlockSpec(memory_space=pl.ANY)] * 2,
        scratch_shapes=[
            f32(n5 * 48 * rows, LANES),
            f32(2, 4, 2, 12, ROWS, LANES),
            f32(4, 2, 12, ROWS, LANES),
            f32(4, 4, 2, 9, ROWS, LANES),
            f32(4, 3, 2, 9, ROWS, LANES),
            f32(2, 12, 32, LANES),
            f32(2, 2, 12, 32, LANES),
            f32(2, 4, 2, 6, ROWS, LANES),
            f32(2, 2, 4, 2, 6, ROWS, LANES),
            f32(2, 2, 4, 2, 6, ROWS, LANES),
            f32(2, 2, 6, 32, LANES),
            sem(2, n5, 3),
            sem(2, n5),
            sem(2),
            sem(2, 4),
            sem(2, 4),
            sem(2, 2, 4),
            sem(2, 2, 4),
            sem(2),
            sem(2),
            sem(2),
        ],
        compiler_params=pltpu.CompilerParams(
            collective_id=0, has_side_effects=True, vmem_limit_bytes=40 * 1024 * 1024
        ),
    )(src, gauge)
    return once.reshape(source_field.shape), twice.reshape(source_field.shape)


def solution(mesh):
    spec = P(None, None, None, "fifth", "st", None)
    return jax.shard_map(
        functools.partial(on_device, mesh.shape["fifth"], mesh.shape["st"]),
        mesh=mesh,
        in_specs=(spec, P(None, None, None, None, "st", "fifth")),
        out_specs=(spec, spec),
        check_vma=False,
    )
```

```python
import functools

import jax
import jax.numpy as jnp
from jax import lax
from jax.experimental import pallas as pl
from jax.experimental.pallas import tpu as pltpu
from jax.sharding import PartitionSpec as P

WALL_HEIGHT = 1.8
QUARK_MASS = 0.5
MESH = pl.DeviceIdType.MESH
LANES = 128
ROWS = 8


def roll(value, shift, axis):
    return pltpu.roll(value, shift % value.shape[axis], axis)


def i_sigma(k, half):
    (r0, r1), (m0, m1) = half
    neg = lambda xs: [-x for x in xs]
    if k == 0:
        return [neg(m1), neg(m0)], [r1, r0]
    if k == 1:
        return [r1, neg(r0)], [m1, neg(m0)]
    return [neg(m0), m1], [r0, neg(r1)]


def combine(a, b, sign):
    op = (lambda x, y: x + y) if sign > 0 else (lambda x, y: x - y)
    return [[[op(x, y) for x, y in zip(sa, sb)] for sa, sb in zip(pa, pb)] for pa, pb in zip(a, b)]


def each(fn, *halves):
    return [
        [[fn(*xs) for xs in zip(*spins)] for spins in zip(*parts)] for parts in zip(*halves)
    ]


def colour_product(link, half, dagger):
    out = [[[None] * 3 for _ in range(2)] for _ in range(2)]
    for a in range(3):
        for b in range(3):
            re = link(0, b, a) if dagger else link(0, a, b)
            im = link(1, b, a) if dagger else link(1, a, b)
            for s in range(2):
                fr, fi = half[0][s][b], half[1][s][b]
                if dagger:
                    tr, ti = re * fr + im * fi, re * fi - im * fr
                else:
                    tr, ti = re * fr - im * fi, re * fi + im * fr
                out[0][s][a] = tr if b == 0 else out[0][s][a] + tr
                out[1][s][a] = ti if b == 0 else out[1][s][a] + ti
    return out


def kernel(n5, nt, rows, src, gauge, once, twice, gath, gath_back, v_buf, part_buf, links, back, stage_in,
           stage_out, fifth_in, time_out, time_in, raw_in,
           gsend, grecv, bsend, brecv, lsem, fsend, frecv, tsend, trecv, rsend, rrecv, osem):
    me = lax.axis_index("fifth")
    mt = lax.axis_index("st")
    nxt, prv = lax.rem(me + 1, n5), lax.rem(me + n5 - 1, n5)
    t_nxt, t_prv = lax.rem(mt + 1, nt), lax.rem(mt + nt - 1, nt)
    q, m = me // 2, lax.rem(me, 2)
    nq = n5 // 2
    pair = q * 2 + 1 - m
    shard_rows = 48 * rows
    half_rows = 24 * rows

    load_src = pltpu.make_async_copy(src, stage_in, lsem.at[0])
    load_src.start()
    load_gauge = pltpu.make_async_copy(
        gauge, gath.at[pl.ds(pl.multiple_of(me * shard_rows, 8), shard_rows)], lsem.at[1]
    )
    load_gauge.start()

    barrier = pltpu.get_barrier_semaphore()
    for peer in (nxt, prv, lax.rem(me + 2, n5), lax.rem(me + n5 - 2, n5)):
        pl.semaphore_signal(barrier, inc=1, device_id={"fifth": peer}, device_id_type=MESH)
    for peer in (t_nxt, t_prv):
        pl.semaphore_signal(barrier, inc=1, device_id={"st": peer}, device_id_type=MESH)
    pl.semaphore_wait(barrier, 6)

    def shard(part, b):
        return gath.at[pl.ds(pl.multiple_of(b * shard_rows + part * half_rows, 8), half_rows)]

    def pass_on(part, b, kind, own=False):
        target = (me + 2, me - 2, pair)[kind]
        return pltpu.make_async_remote_copy(
            src_ref=gauge.at[pl.ds(part * half_rows, half_rows)] if own else shard(part, b),
            dst_ref=shard(part, b),
            send_sem=gsend.at[part, b, kind],
            recv_sem=grecv.at[part, b],
            device_id={"fifth": target},
            device_id_type=MESH,
        )

    time_rows = -(-6 * rows // 8) * 8

    def time_rows_on(part, b, own=False):
        first = part * half_rows + half_rows - time_rows
        span = pl.ds(pl.multiple_of(b * shard_rows + first, 8), time_rows)
        return pltpu.make_async_remote_copy(
            src_ref=gauge.at[pl.ds(first, time_rows)] if own else gath.at[span],
            dst_ref=gath_back.at[span],
            send_sem=bsend.at[part, b],
            recv_sem=brecv.at[part, b],
            device_id={"st": t_nxt},
            device_id_type=MESH,
        )

    def arrived(part, b):
        pass_on(part, b, 2).wait_recv()

    has_up, has_down = q + 1 < nq, q > 0

    pass_on(1, me, 2, True).start()
    pass_on(0, me, 2, True).start()

    @pl.when(has_up)
    def _():
        pass_on(0, me, 0, True).start()
        pass_on(1, me, 0, True).start()

    @pl.when(has_down)
    def _():
        pass_on(0, me, 1, True).start()
        pass_on(1, me, 1, True).start()

    time_rows_on(0, me, True).start()
    time_rows_on(1, me, True).start()

    def raw_copy(which):
        return pltpu.make_async_remote_copy(
            src_ref=src.at[:, pl.ds(6 * which, 6)],
            dst_ref=raw_in.at[which],
            send_sem=rsend.at[which],
            recv_sem=rrecv.at[which],
            device_id={"fifth": (nxt, prv)[which]},
            device_id_type=MESH,
        )

    raw_copy(0).start()
    raw_copy(1).start()

    def fifth_copy(which, j):
        return pltpu.make_async_remote_copy(
            src_ref=v_buf.at[1, j, :, pl.ds(6 * which, 6)],
            dst_ref=fifth_in.at[which, j],
            send_sem=fsend.at[which, j],
            recv_sem=frecv.at[which, j],
            device_id={"fifth": (nxt, prv)[which]},
            device_id_type=MESH,
        )

    def time_copy(phase, which, j):
        return pltpu.make_async_remote_copy(
            src_ref=time_out.at[phase, which, j],
            dst_ref=time_in.at[phase, which, j],
            send_sem=tsend.at[phase, which, j],
            recv_sem=trecv.at[phase, which, j],
            device_id={"st": (t_prv, t_nxt)[which]},
            device_id_type=MESH,
        )

    def load_half(ref, base):
        return [[[ref(p, base + 3 * s + c) for c in range(3)] for s in range(2)] for p in range(2)]

    def put_half(ref, half):
        for p in range(2):
            for s in range(2):
                for c in range(3):
                    ref[p, 3 * s + c] = half[p][s][c]

    load_src.wait()

    @pl.loop(0, 4)
    def _(j):
        for p in range(2):
            for c in range(12):
                v_buf[0, j, p, c] = stage_in[p, c, pl.ds(j, ROWS, stride=4), :]
        get = lambda p, c: v_buf[0, j, p, c]
        put_half(time_out.at[0, 0, j], combine(load_half(get, 0), load_half(get, 6), -1))
        put_half(time_out.at[0, 1, j], combine(load_half(get, 0), load_half(get, 6), 1))
        time_copy(0, 0, j).start()
        time_copy(0, 1, j).start()

    arrived(1, pair)

    @pl.when(has_up)
    def _():
        pass_on(1, pair, 0).start()

    @pl.when(has_down)
    def _():
        pass_on(1, pair, 1).start()

    time_rows_on(1, pair).start()

    @pl.loop(1, nq)
    def _(k):
        below, above = me - 2 * k, me + 2 * k
        pair_below, pair_above = pair - 2 * k, pair + 2 * k

        @pl.when(q - k >= 0)
        def _():
            arrived(0, below)

            @pl.when(has_up)
            def _():
                pass_on(0, below, 0).start()

            pass_on(0, below, 2).start()
            time_rows_on(0, below).start()

        @pl.when(q + k < nq)
        def _():
            arrived(0, above)

            @pl.when(has_down)
            def _():
                pass_on(0, above, 1).start()

            pass_on(0, above, 2).start()
            time_rows_on(0, above).start()

        for b_low, b_high in ((below, above), (pair_below, pair_above)):

            @pl.when(q - k >= 0)
            def _():
                arrived(1, b_low)

                @pl.when(has_up)
                def _():
                    pass_on(1, b_low, 0).start()

                time_rows_on(1, b_low).start()

            @pl.when(q + k < nq)
            def _():
                arrived(1, b_high)

                @pl.when(has_down)
                def _():
                    pass_on(1, b_high, 1).start()

                time_rows_on(1, b_high).start()

    @pl.loop(0, nq)
    def _(k):
        arrived(0, 2 * k + 1 - m)
        time_rows_on(0, 2 * k + 1 - m).start()

    load_gauge.wait()

    def complete(source, j, mu, slot):
        offset = (j // rows) * shard_rows + lax.rem(j, rows)
        u = [[[None] * 3 for _ in range(3)] for _ in range(2)]
        for p in range(2):
            for a in range(2):
                for b in range(3):
                    comp = ((p * 4 + mu) * 2 + a) * 3 + b
                    u[p][a][b] = source[pl.ds(offset + comp * rows, ROWS, stride=192), :]
        (r0, r1, _), (m0, m1, _) = u
        for a in range(3):
            b, c = (a + 1) % 3, (a + 2) % 3
            u[0][2][a] = (r0[b] * r1[c] - m0[b] * m1[c]) - (r0[c] * r1[b] - m0[c] * m1[b])
            u[1][2][a] = (r0[c] * m1[b] + m0[c] * r1[b]) - (r0[b] * m1[c] + m0[b] * r1[c])
        for p in range(2):
            for a in range(3):
                for b in range(3):
                    links[j, slot, p, 3 * a + b] = u[p][a][b]

    @pl.loop(0, 4)
    def _(j):
        for mu in range(4):
            complete(gath, j, mu, mu)

    lane = lax.broadcasted_iota(jnp.int32, (ROWS, LANES), 1)
    x = lax.rem(lane, 16)

    def xor1(j):
        return j + 1 - 2 * lax.rem(j, 2)

    def xor2(j):
        return lax.rem(j + 2, 4)

    def shift(k, ahead, j, here, there):
        if k == 0:
            if ahead:
                return jnp.where(x == 15, roll(here, 15, 1), roll(here, -1, 1))
            return jnp.where(x == 0, roll(here, -15, 1), roll(here, 1, 1))
        if k == 1:
            if ahead:
                return roll(jnp.where(lane >= 16, here, there), -16, 1)
            return roll(jnp.where(lane < LANES - 16, here, there), 16, 1)
        if ahead:
            return jnp.where(j >= 2, roll(there, -1, 0), there)
        return jnp.where(j < 2, roll(there, 1, 0), there)

    @pl.loop(0, 4)
    def _(j):
        other = (j, xor1(j), xor2(j))
        for k in range(3):
            for p in range(2):
                for c in range(9):
                    back[j, k, p, c] = shift(
                        k, False, j, links[j, k, p, c], links[other[k], k, p, c]
                    )

    time_last = jnp.where(mt == nt - 1, -1.0, 1.0).astype(jnp.float32)
    time_first = jnp.where(mt == 0, -1.0, 1.0).astype(jnp.float32)
    fifth_last = jnp.where(me == n5 - 1, -QUARK_MASS, 1.0).astype(jnp.float32)
    fifth_first = jnp.where(me == 0, -QUARK_MASS, 1.0).astype(jnp.float32)

    def local_part(phase):
        @pl.loop(0, 4)
        def _(j):
            other = (j, xor1(j), xor2(j))
            for k in range(3):

                def halves(at):
                    get = lambda p, c: v_buf[phase, at, p, c]
                    upper, turned = load_half(get, 0), i_sigma_lists(k, load_half(get, 6))
                    return combine(upper, turned, 1), combine(upper, turned, -1)

                there_plus, there_minus = halves(other[k])
                here_plus, here_minus = halves(j) if k == 1 else (there_plus, there_minus)
                go = lambda ahead: lambda h, t: shift(k, ahead, j, h, t)
                ahead_half = each(go(True), here_plus, there_plus)
                behind_half = each(go(False), here_minus, there_minus)
                moved_ahead = colour_product(
                    lambda p, a, b: links[j, k, p, 3 * a + b], ahead_half, False
                )
                moved_behind = colour_product(
                    lambda p, a, b: back[j, k, p, 3 * a + b], behind_half, True
                )
                upper = combine(moved_ahead, moved_behind, 1)
                lower = i_sigma_lists(k, combine(moved_behind, moved_ahead, -1))
                for base, half in ((0, upper), (6, lower)):
                    for p in range(2):
                        for s in range(2):
                            for c in range(3):
                                i = base + 3 * s + c
                                old = (
                                    (5.0 - WALL_HEIGHT) * v_buf[phase, j, p, i]
                                    if k == 0
                                    else part_buf[j, p, i]
                                )
                                part_buf[j, p, i] = old - 0.5 * half[p][s][c]

    def finish(phase):
        @pl.loop(0, 4)
        def _(j):
            time_copy(phase, 0, j).wait_recv()
            time_copy(phase, 1, j).wait_recv()
            if phase == 1:
                fifth_copy(0, j).wait_recv()
                fifth_copy(1, j).wait_recv()
            ahead = load_half(lambda p, c: time_in[phase, 0, j, p, c] * time_last, 0)
            behind = load_half(lambda p, c: time_in[phase, 1, j, p, c] * time_first, 0)
            moved = colour_product(lambda p, a, b: links[j, 3, p, 3 * a + b], ahead, False)
            behind = colour_product(lambda p, a, b: links[j, 4, p, 3 * a + b], behind, True)
            upper = combine(moved, behind, 1)
            lower = combine(behind, moved, -1)
            for which, half in ((0, upper), (1, lower)):
                for p in range(2):
                    for s in range(2):
                        for c in range(3):
                            i = 3 * s + c
                            if phase == 0:
                                chiral = raw_in[which, p, i, pl.ds(j, ROWS, stride=4), :]
                            else:
                                chiral = fifth_in[which, j, p, i]
                            chiral = chiral * (fifth_first, fifth_last)[which]
                            value = part_buf[j, p, 6 * which + i] - 0.5 * half[p][s][c] - chiral
                            stage_out[phase, p, 6 * which + i, pl.ds(j, ROWS, stride=4), :] = value
                            if phase == 0:
                                v_buf[1, j, p, 6 * which + i] = value
            if phase == 0:
                fifth_copy(0, j).start()
                fifth_copy(1, j).start()
                get = lambda p, c: v_buf[1, j, p, c]
                put_half(time_out.at[1, 0, j], combine(load_half(get, 0), load_half(get, 6), -1))
                time_copy(1, 0, j).start()
                put_half(time_out.at[1, 1, j], combine(load_half(get, 0), load_half(get, 6), 1))
                time_copy(1, 1, j).start()

    local_part(0)

    @pl.loop(0, n5)
    def _(b):
        time_rows_on(0, b).wait_recv()
        time_rows_on(1, b).wait_recv()

    @pl.loop(0, 4)
    def _(j):
        complete(gath_back, j, 3, 4)

    raw_copy(0).wait_recv()
    raw_copy(1).wait_recv()
    finish(0)
    write_once = pltpu.make_async_copy(stage_out.at[0], once, osem.at[0])
    write_once.start()
    local_part(1)
    finish(1)
    write_twice = pltpu.make_async_copy(stage_out.at[1], twice, osem.at[1])
    write_twice.start()

    raw_copy(0).wait_send()
    raw_copy(1).wait_send()

    @pl.loop(0, 4)
    def _(j):
        for which in range(2):
            fifth_copy(which, j).wait_send()
            time_copy(0, which, j).wait_send()
            time_copy(1, which, j).wait_send()

    @pl.loop(0, n5)
    def _(b):
        time_rows_on(0, b).wait_send()
        time_rows_on(1, b).wait_send()

    for b in (me, pair):

        @pl.when(has_up)
        def _():
            pass_on(1, b, 0).wait_send()

        @pl.when(has_down)
        def _():
            pass_on(1, b, 1).wait_send()

    pass_on(1, me, 2).wait_send()
    pass_on(0, me, 2).wait_send()

    @pl.when(has_up)
    def _():
        pass_on(0, me, 0).wait_send()

    @pl.when(has_down)
    def _():
        pass_on(0, me, 1).wait_send()

    @pl.loop(1, nq)
    def _(k):
        below, above = me - 2 * k, me + 2 * k
        pair_below, pair_above = pair - 2 * k, pair + 2 * k

        @pl.when(q - k >= 0)
        def _():
            pass_on(0, below, 2).wait_send()

            @pl.when(has_up)
            def _():
                pass_on(0, below, 0).wait_send()
                pass_on(1, below, 0).wait_send()
                pass_on(1, pair_below, 0).wait_send()

        @pl.when(q + k < nq)
        def _():
            pass_on(0, above, 2).wait_send()

            @pl.when(has_down)
            def _():
                pass_on(0, above, 1).wait_send()
                pass_on(1, above, 1).wait_send()
                pass_on(1, pair_above, 1).wait_send()

    write_once.wait()
    write_twice.wait()


def i_sigma_lists(k, half):
    return [list(part) for part in i_sigma(k, half)]


def on_device(n5, nt, source_field, gauge_rows):
    rows = gauge_rows.shape[-1] // LANES
    src = source_field.reshape(2, 12, 32, LANES)
    gauge = gauge_rows.reshape(48 * rows, LANES)
    field = jax.ShapeDtypeStruct((2, 12, 32, LANES), jnp.float32)
    f32 = lambda *shape: pltpu.VMEM(shape, jnp.float32)
    sem = lambda *shape: pltpu.SemaphoreType.DMA(shape)
    once, twice = pl.pallas_call(
        functools.partial(kernel, n5, nt, rows),
        out_shape=(field, field),
        in_specs=[pl.BlockSpec(memory_space=pl.ANY)] * 2,
        out_specs=[pl.BlockSpec(memory_space=pl.ANY)] * 2,
        scratch_shapes=[
            f32(n5 * 48 * rows, LANES),
            f32(n5 * 48 * rows, LANES),
            f32(2, 4, 2, 12, ROWS, LANES),
            f32(4, 2, 12, ROWS, LANES),
            f32(4, 5, 2, 9, ROWS, LANES),
            f32(4, 3, 2, 9, ROWS, LANES),
            f32(2, 12, 32, LANES),
            f32(2, 2, 12, 32, LANES),
            f32(2, 4, 2, 6, ROWS, LANES),
            f32(2, 2, 4, 2, 6, ROWS, LANES),
            f32(2, 2, 4, 2, 6, ROWS, LANES),
            f32(2, 2, 6, 32, LANES),
            sem(2, n5, 3),
            sem(2, n5),
            sem(2, n5),
            sem(2, n5),
            sem(2),
            sem(2, 4),
            sem(2, 4),
            sem(2, 2, 4),
            sem(2, 2, 4),
            sem(2),
            sem(2),
            sem(2),
        ],
        compiler_params=pltpu.CompilerParams(
            collective_id=0, has_side_effects=True, vmem_limit_bytes=66187264
        ),
    )(src, gauge)
    return once.reshape(source_field.shape), twice.reshape(source_field.shape)


def solution(mesh):
    spec = P(None, None, None, "fifth", "st", None)
    return jax.shard_map(
        functools.partial(on_device, mesh.shape["fifth"], mesh.shape["st"]),
        mesh=mesh,
        in_specs=(spec, P(None, None, None, None, "st", "fifth")),
        out_specs=(spec, spec),
        check_vma=False,
    )
```

```python
import functools

import jax
import jax.numpy as jnp
from jax import lax
from jax.experimental import pallas as pl
from jax.experimental.pallas import tpu as pltpu
from jax.sharding import PartitionSpec as P

WALL_HEIGHT = 1.8
QUARK_MASS = 0.5
MESH = pl.DeviceIdType.MESH
LANES = 128
ROWS = 8


def roll(value, shift, axis):
    return pltpu.roll(value, shift % value.shape[axis], axis)


def i_sigma(k, half):
    (r0, r1), (m0, m1) = half
    neg = lambda xs: [-x for x in xs]
    if k == 0:
        return [neg(m1), neg(m0)], [r1, r0]
    if k == 1:
        return [r1, neg(r0)], [m1, neg(m0)]
    return [neg(m0), m1], [r0, neg(r1)]


def combine(a, b, sign):
    op = (lambda x, y: x + y) if sign > 0 else (lambda x, y: x - y)
    return [[[op(x, y) for x, y in zip(sa, sb)] for sa, sb in zip(pa, pb)] for pa, pb in zip(a, b)]


def each(fn, *halves):
    return [
        [[fn(*xs) for xs in zip(*spins)] for spins in zip(*parts)] for parts in zip(*halves)
    ]


def colour_product(link, half, dagger):
    out = [[[None] * 3 for _ in range(2)] for _ in range(2)]
    for a in range(3):
        for b in range(3):
            re = link(0, b, a) if dagger else link(0, a, b)
            im = link(1, b, a) if dagger else link(1, a, b)
            for s in range(2):
                fr, fi = half[0][s][b], half[1][s][b]
                if dagger:
                    tr, ti = re * fr + im * fi, re * fi - im * fr
                else:
                    tr, ti = re * fr - im * fi, re * fi + im * fr
                out[0][s][a] = tr if b == 0 else out[0][s][a] + tr
                out[1][s][a] = ti if b == 0 else out[1][s][a] + ti
    return out


def kernel(n5, nt, rows, src, gauge, once, twice, gath, gath_back, v_buf, part_buf, links, back, stage_in,
           stage_out, fifth_in, time_out, time_in, raw_in,
           gsend, grecv, bsend, brecv, lsem, fsend, frecv, tsend, trecv, rsend, rrecv, osem):
    me = lax.axis_index("fifth")
    mt = lax.axis_index("st")
    nxt, prv = lax.rem(me + 1, n5), lax.rem(me + n5 - 1, n5)
    t_nxt, t_prv = lax.rem(mt + 1, nt), lax.rem(mt + nt - 1, nt)
    q, m = me // 2, lax.rem(me, 2)
    nq = n5 // 2
    pair = q * 2 + 1 - m
    shard_rows = 48 * rows
    half_rows = 24 * rows

    load_src = pltpu.make_async_copy(src, stage_in, lsem.at[0])
    load_src.start()
    load_gauge = pltpu.make_async_copy(
        gauge, gath.at[pl.ds(pl.multiple_of(me * shard_rows, 8), shard_rows)], lsem.at[1]
    )
    load_gauge.start()

    barrier = pltpu.get_barrier_semaphore()
    for peer in (nxt, prv, lax.rem(me + 2, n5), lax.rem(me + n5 - 2, n5)):
        pl.semaphore_signal(barrier, inc=1, device_id={"fifth": peer}, device_id_type=MESH)
    for peer in (t_nxt, t_prv):
        pl.semaphore_signal(barrier, inc=1, device_id={"st": peer}, device_id_type=MESH)
    pl.semaphore_wait(barrier, 6)

    def shard(part, b):
        return gath.at[pl.ds(pl.multiple_of(b * shard_rows + part * half_rows, 8), half_rows)]

    def pass_on(part, b, kind, own=False):
        target = (me + 2, me - 2, pair)[kind]
        return pltpu.make_async_remote_copy(
            src_ref=gauge.at[pl.ds(part * half_rows, half_rows)] if own else shard(part, b),
            dst_ref=shard(part, b),
            send_sem=gsend.at[part, b, kind],
            recv_sem=grecv.at[part, b],
            device_id={"fifth": target},
            device_id_type=MESH,
        )

    time_rows = -(-6 * rows // 8) * 8

    def time_rows_on(part, b, own=False):
        first = part * half_rows + half_rows - time_rows
        span = pl.ds(pl.multiple_of(b * shard_rows + first, 8), time_rows)
        return pltpu.make_async_remote_copy(
            src_ref=gauge.at[pl.ds(first, time_rows)] if own else gath.at[span],
            dst_ref=gath_back.at[span],
            send_sem=bsend.at[part, b],
            recv_sem=brecv.at[part, b],
            device_id={"st": t_nxt},
            device_id_type=MESH,
        )

    def arrived(part, b):
        pass_on(part, b, 2).wait_recv()

    has_up, has_down = q + 1 < nq, q > 0

    pass_on(1, me, 2, True).start()
    pass_on(0, me, 2, True).start()

    @pl.when(has_up)
    def _():
        pass_on(0, me, 0, True).start()
        pass_on(1, me, 0, True).start()

    @pl.when(has_down)
    def _():
        pass_on(0, me, 1, True).start()
        pass_on(1, me, 1, True).start()

    time_rows_on(0, me, True).start()
    time_rows_on(1, me, True).start()

    def raw_copy(which):
        return pltpu.make_async_remote_copy(
            src_ref=src.at[:, pl.ds(6 * which, 6)],
            dst_ref=raw_in.at[which],
            send_sem=rsend.at[which],
            recv_sem=rrecv.at[which],
            device_id={"fifth": (nxt, prv)[which]},
            device_id_type=MESH,
        )

    raw_copy(0).start()
    raw_copy(1).start()

    def fifth_copy(which, j):
        return pltpu.make_async_remote_copy(
            src_ref=v_buf.at[1, j, :, pl.ds(6 * which, 6)],
            dst_ref=fifth_in.at[which, j],
            send_sem=fsend.at[which, j],
            recv_sem=frecv.at[which, j],
            device_id={"fifth": (nxt, prv)[which]},
            device_id_type=MESH,
        )

    def time_copy(phase, which, j):
        return pltpu.make_async_remote_copy(
            src_ref=time_out.at[phase, which, j],
            dst_ref=time_in.at[phase, which, j],
            send_sem=tsend.at[phase, which, j],
            recv_sem=trecv.at[phase, which, j],
            device_id={"st": (t_prv, t_nxt)[which]},
            device_id_type=MESH,
        )

    def load_half(ref, base):
        return [[[ref(p, base + 3 * s + c) for c in range(3)] for s in range(2)] for p in range(2)]

    def put_half(ref, half):
        for p in range(2):
            for s in range(2):
                for c in range(3):
                    ref[p, 3 * s + c] = half[p][s][c]

    load_src.wait()

    @pl.loop(0, 4)
    def _(j):
        for p in range(2):
            for c in range(12):
                v_buf[0, j, p, c] = stage_in[p, c, pl.ds(j, ROWS, stride=4), :]
        get = lambda p, c: v_buf[0, j, p, c]
        put_half(time_out.at[0, 0, j], combine(load_half(get, 0), load_half(get, 6), -1))
        put_half(time_out.at[0, 1, j], combine(load_half(get, 0), load_half(get, 6), 1))
        time_copy(0, 0, j).start()
        time_copy(0, 1, j).start()

    arrived(1, pair)

    @pl.when(has_up)
    def _():
        pass_on(1, pair, 0).start()

    @pl.when(has_down)
    def _():
        pass_on(1, pair, 1).start()

    time_rows_on(1, pair).start()

    @pl.loop(1, nq)
    def _(k):
        below, above = me - 2 * k, me + 2 * k
        pair_below, pair_above = pair - 2 * k, pair + 2 * k

        @pl.when(q - k >= 0)
        def _():
            arrived(0, below)

            @pl.when(has_up)
            def _():
                pass_on(0, below, 0).start()

            pass_on(0, below, 2).start()
            time_rows_on(0, below).start()

        @pl.when(q + k < nq)
        def _():
            arrived(0, above)

            @pl.when(has_down)
            def _():
                pass_on(0, above, 1).start()

            pass_on(0, above, 2).start()
            time_rows_on(0, above).start()

        for b_low, b_high in ((below, above), (pair_below, pair_above)):

            @pl.when(q - k >= 0)
            def _():
                arrived(1, b_low)

                @pl.when(has_up)
                def _():
                    pass_on(1, b_low, 0).start()

                time_rows_on(1, b_low).start()

            @pl.when(q + k < nq)
            def _():
                arrived(1, b_high)

                @pl.when(has_down)
                def _():
                    pass_on(1, b_high, 1).start()

                time_rows_on(1, b_high).start()

    @pl.loop(0, nq)
    def _(k):
        arrived(0, 2 * k + 1 - m)
        time_rows_on(0, 2 * k + 1 - m).start()

    load_gauge.wait()

    def complete(source, j, mu, slot):
        offset = (j // rows) * shard_rows + lax.rem(j, rows)
        u = [[[None] * 3 for _ in range(3)] for _ in range(2)]
        for p in range(2):
            for a in range(2):
                for b in range(3):
                    comp = ((p * 4 + mu) * 2 + a) * 3 + b
                    u[p][a][b] = source[pl.ds(offset + comp * rows, ROWS, stride=192), :]
        (r0, r1, _), (m0, m1, _) = u
        for a in range(3):
            b, c = (a + 1) % 3, (a + 2) % 3
            u[0][2][a] = (r0[b] * r1[c] - m0[b] * m1[c]) - (r0[c] * r1[b] - m0[c] * m1[b])
            u[1][2][a] = (r0[c] * m1[b] + m0[c] * r1[b]) - (r0[b] * m1[c] + m0[b] * r1[c])
        for p in range(2):
            for a in range(3):
                for b in range(3):
                    links[j, slot, p, 3 * a + b] = u[p][a][b]

    @pl.loop(0, 4)
    def _(j):
        for mu in range(4):
            complete(gath, j, mu, mu)

    lane = lax.broadcasted_iota(jnp.int32, (ROWS, LANES), 1)
    x = lax.rem(lane, 16)

    def xor1(j):
        return j + 1 - 2 * lax.rem(j, 2)

    def xor2(j):
        return lax.rem(j + 2, 4)

    def shift(k, ahead, j, here, there):
        if k == 0:
            if ahead:
                return jnp.where(x == 15, roll(here, 15, 1), roll(here, -1, 1))
            return jnp.where(x == 0, roll(here, -15, 1), roll(here, 1, 1))
        if k == 1:
            if ahead:
                return roll(jnp.where(lane >= 16, here, there), -16, 1)
            return roll(jnp.where(lane < LANES - 16, here, there), 16, 1)
        if ahead:
            return jnp.where(j >= 2, roll(there, -1, 0), there)
        return jnp.where(j < 2, roll(there, 1, 0), there)

    @pl.loop(0, 4)
    def _(j):
        other = (j, xor1(j), xor2(j))
        for k in range(3):
            for p in range(2):
                for c in range(9):
                    back[j, k, p, c] = shift(
                        k, False, j, links[j, k, p, c], links[other[k], k, p, c]
                    )

    time_last = jnp.where(mt == nt - 1, -1.0, 1.0).astype(jnp.float32)
    time_first = jnp.where(mt == 0, -1.0, 1.0).astype(jnp.float32)
    fifth_last = jnp.where(me == n5 - 1, -QUARK_MASS, 1.0).astype(jnp.float32)
    fifth_first = jnp.where(me == 0, -QUARK_MASS, 1.0).astype(jnp.float32)

    def local_part(phase):
        @pl.loop(0, 4)
        def _(j):
            other = (j, xor1(j), xor2(j))
            for k in range(3):

                def halves(at):
                    get = lambda p, c: v_buf[phase, at, p, c]
                    upper, turned = load_half(get, 0), i_sigma_lists(k, load_half(get, 6))
                    return combine(upper, turned, 1), combine(upper, turned, -1)

                there_plus, there_minus = halves(other[k])
                here_plus, here_minus = halves(j) if k == 1 else (there_plus, there_minus)
                go = lambda ahead: lambda h, t: shift(k, ahead, j, h, t)
                ahead_half = each(go(True), here_plus, there_plus)
                behind_half = each(go(False), here_minus, there_minus)
                moved_ahead = colour_product(
                    lambda p, a, b: links[j, k, p, 3 * a + b], ahead_half, False
                )
                moved_behind = colour_product(
                    lambda p, a, b: back[j, k, p, 3 * a + b], behind_half, True
                )
                upper = combine(moved_ahead, moved_behind, 1)
                lower = i_sigma_lists(k, combine(moved_behind, moved_ahead, -1))
                for base, half in ((0, upper), (6, lower)):
                    for p in range(2):
                        for s in range(2):
                            for c in range(3):
                                i = base + 3 * s + c
                                old = (
                                    (5.0 - WALL_HEIGHT) * v_buf[phase, j, p, i]
                                    if k == 0
                                    else part_buf[j, p, i]
                                )
                                part_buf[j, p, i] = old - 0.5 * half[p][s][c]

    def finish(phase):
        @pl.loop(0, 4)
        def _(j):
            time_copy(phase, 0, j).wait_recv()
            time_copy(phase, 1, j).wait_recv()
            if phase == 1:
                fifth_copy(0, j).wait_recv()
                fifth_copy(1, j).wait_recv()
            ahead = load_half(lambda p, c: time_in[phase, 0, j, p, c] * time_last, 0)
            behind = load_half(lambda p, c: time_in[phase, 1, j, p, c] * time_first, 0)
            moved = colour_product(lambda p, a, b: links[j, 3, p, 3 * a + b], ahead, False)
            behind = colour_product(lambda p, a, b: links[j, 4, p, 3 * a + b], behind, True)
            upper = combine(moved, behind, 1)
            lower = combine(behind, moved, -1)
            for which, half in ((0, upper), (1, lower)):
                for p in range(2):
                    for s in range(2):
                        for c in range(3):
                            i = 3 * s + c
                            if phase == 0:
                                chiral = raw_in[which, p, i, pl.ds(j, ROWS, stride=4), :]
                            else:
                                chiral = fifth_in[which, j, p, i]
                            chiral = chiral * (fifth_first, fifth_last)[which]
                            value = part_buf[j, p, 6 * which + i] - 0.5 * half[p][s][c] - chiral
                            stage_out[phase, p, 6 * which + i, pl.ds(j, ROWS, stride=4), :] = value
                            if phase == 0:
                                v_buf[1, j, p, 6 * which + i] = value
                if phase == 0:
                    fifth_copy(which, j).start()
            if phase == 0:
                get = lambda p, c: v_buf[1, j, p, c]
                put_half(time_out.at[1, 0, j], combine(load_half(get, 0), load_half(get, 6), -1))
                time_copy(1, 0, j).start()
                put_half(time_out.at[1, 1, j], combine(load_half(get, 0), load_half(get, 6), 1))
                time_copy(1, 1, j).start()

    local_part(0)

    @pl.loop(0, n5)
    def _(b):
        time_rows_on(0, b).wait_recv()
        time_rows_on(1, b).wait_recv()

    @pl.loop(0, 4)
    def _(j):
        complete(gath_back, j, 3, 4)

    raw_copy(0).wait_recv()
    raw_copy(1).wait_recv()
    finish(0)
    write_once = pltpu.make_async_copy(stage_out.at[0], once, osem.at[0])
    write_once.start()
    local_part(1)
    finish(1)
    write_twice = pltpu.make_async_copy(stage_out.at[1], twice, osem.at[1])
    write_twice.start()

    raw_copy(0).wait_send()
    raw_copy(1).wait_send()

    @pl.loop(0, 4)
    def _(j):
        for which in range(2):
            fifth_copy(which, j).wait_send()
            time_copy(0, which, j).wait_send()
            time_copy(1, which, j).wait_send()

    @pl.loop(0, n5)
    def _(b):
        time_rows_on(0, b).wait_send()
        time_rows_on(1, b).wait_send()

    for b in (me, pair):

        @pl.when(has_up)
        def _():
            pass_on(1, b, 0).wait_send()

        @pl.when(has_down)
        def _():
            pass_on(1, b, 1).wait_send()

    pass_on(1, me, 2).wait_send()
    pass_on(0, me, 2).wait_send()

    @pl.when(has_up)
    def _():
        pass_on(0, me, 0).wait_send()

    @pl.when(has_down)
    def _():
        pass_on(0, me, 1).wait_send()

    @pl.loop(1, nq)
    def _(k):
        below, above = me - 2 * k, me + 2 * k
        pair_below, pair_above = pair - 2 * k, pair + 2 * k

        @pl.when(q - k >= 0)
        def _():
            pass_on(0, below, 2).wait_send()

            @pl.when(has_up)
            def _():
                pass_on(0, below, 0).wait_send()
                pass_on(1, below, 0).wait_send()
                pass_on(1, pair_below, 0).wait_send()

        @pl.when(q + k < nq)
        def _():
            pass_on(0, above, 2).wait_send()

            @pl.when(has_down)
            def _():
                pass_on(0, above, 1).wait_send()
                pass_on(1, above, 1).wait_send()
                pass_on(1, pair_above, 1).wait_send()

    write_once.wait()
    write_twice.wait()


def i_sigma_lists(k, half):
    return [list(part) for part in i_sigma(k, half)]


def on_device(n5, nt, source_field, gauge_rows):
    rows = gauge_rows.shape[-1] // LANES
    src = source_field.reshape(2, 12, 32, LANES)
    gauge = gauge_rows.reshape(48 * rows, LANES)
    field = jax.ShapeDtypeStruct((2, 12, 32, LANES), jnp.float32)
    f32 = lambda *shape: pltpu.VMEM(shape, jnp.float32)
    sem = lambda *shape: pltpu.SemaphoreType.DMA(shape)
    once, twice = pl.pallas_call(
        functools.partial(kernel, n5, nt, rows),
        out_shape=(field, field),
        in_specs=[pl.BlockSpec(memory_space=pl.ANY)] * 2,
        out_specs=[pl.BlockSpec(memory_space=pl.ANY)] * 2,
        scratch_shapes=[
            f32(n5 * 48 * rows, LANES),
            f32(n5 * 48 * rows, LANES),
            f32(2, 4, 2, 12, ROWS, LANES),
            f32(4, 2, 12, ROWS, LANES),
            f32(4, 5, 2, 9, ROWS, LANES),
            f32(4, 3, 2, 9, ROWS, LANES),
            f32(2, 12, 32, LANES),
            f32(2, 2, 12, 32, LANES),
            f32(2, 4, 2, 6, ROWS, LANES),
            f32(2, 2, 4, 2, 6, ROWS, LANES),
            f32(2, 2, 4, 2, 6, ROWS, LANES),
            f32(2, 2, 6, 32, LANES),
            sem(2, n5, 3),
            sem(2, n5),
            sem(2, n5),
            sem(2, n5),
            sem(2),
            sem(2, 4),
            sem(2, 4),
            sem(2, 2, 4),
            sem(2, 2, 4),
            sem(2),
            sem(2),
            sem(2),
        ],
        compiler_params=pltpu.CompilerParams(
            collective_id=0, has_side_effects=True, vmem_limit_bytes=66187264
        ),
    )(src, gauge)
    return once.reshape(source_field.shape), twice.reshape(source_field.shape)


def solution(mesh):
    spec = P(None, None, None, "fifth", "st", None)
    return jax.shard_map(
        functools.partial(on_device, mesh.shape["fifth"], mesh.shape["st"]),
        mesh=mesh,
        in_specs=(spec, P(None, None, None, None, "st", "fifth")),
        out_specs=(spec, spec),
        check_vma=False,
    )
```
